32 devices in a mesh: row: 4 (over y, core), col: 8 (over z, x).
Axes of the slice: x: 2, y: 2, z: 4, core: 2. Of those that a mesh axis runs over, the one named last changes fastest.
Arguments:
- density: float32 [8192, 8192], P('row', 'col'), may hold values from -4 to 4
- block_mask: int32 [64, 64], P('row', 'col'), may hold values from 0 to 1, as said below
- keep_mask: int32 [64, 64], P('row', 'col'), may hold values 0 or 1
- owner: int32 [4096], P(('row', 'col')), may hold values from 0 to 31, as said below
Outputs:
- owned: float32 [4096, 128, 128], P(('row', 'col'))
The draws below stay inside these ranges and needn't reach their ends.
Inputs may be any that keep to these rules, and one draw needn't show every extreme that they name: `block_mask`: each aligned square of 8 x 8 blocks holds exactly 8 ones. Every device owns exactly 128 blocks; of the 128 blocks listed at t * 128 to t * 128 + 127, at most 4 share one owner, and some owner takes exactly 4 of them.
All inputs are finite; a program needn't handle non-finite values. No bound on the sum of `keep_mask` on one device may be relied on, other than what follows from the above.
Results may differ from the reference program's by a relative error of at most 0.0001.
Values sent between devices are 32-bit elements; how exact they have to be, the bound alone decides.
No kernel may reach another device: no remote copies, remote signals or barrier semaphores. Data moves between devices by JAX's collectives and lax.ppermute only.
A program may use at most 192 MiB of HBM per device.

```python
import jax
import jax.numpy as jnp
from jax import lax

BLK = 128
BC = 8
BR = 16
NB = 64
TILE = 128
NZS = 8
GROUPS = 32
N_ROW = 4
N_COL = 8
DEVICES = 32


def draw_block_mask(key, part):
    squares = NB // BC
    cells = BC * BC
    scores = jax.random.randint(key, (squares, squares, cells), 0, 2 ** 20) * cells + jnp.arange(cells, dtype=jnp.int32)
    ranks = jnp.argsort(jnp.argsort(scores, axis=-1), axis=-1)
    chosen = (ranks < NZS).astype(jnp.int32)
    return chosen.reshape(squares, squares, BC, BC).transpose(0, 2, 1, 3).reshape(NB, NB)


def shuffle_tile(subkey):
    return jax.random.permutation(subkey, TILE)


def draw_owner(key, part):
    first, second, third = jax.random.split(key, 3)
    offsets = jax.random.permutation(first, DEVICES)[:GROUPS]
    groups = jnp.arange(TILE, dtype=jnp.int32) * GROUPS // TILE
    shifts = offsets[groups]
    orders = jax.vmap(shuffle_tile)(jax.random.split(second, DEVICES))
    receivers = jax.random.permutation(third, DEVICES)
    tiles = jnp.arange(DEVICES, dtype=jnp.int32)[:, None]
    return receivers[(tiles + shifts[orders]) % DEVICES].reshape(-1).astype(jnp.int32)


def place_ends(result, stream_key, low, top_value):
    shape = result.shape
    spot = [jax.random.randint(jax.random.fold_in(stream_key, axis), (), 0, shape[axis]) for axis in range(len(shape))]
    result = result.at[tuple(spot)].set(low)
    longest = shape.index(max(shape))
    spot[longest] = (spot[longest] + 1) % shape[longest]
    return result.at[tuple(spot)].set(top_value)


def steps_of(key, shape, cuts, low, top_value):
    loudness = 1.0
    for dim, shards_of in cuts:
        heights = jax.random.uniform(jax.random.fold_in(jax.random.fold_in(key, 6), dim), (shards_of,), jnp.float32, low / len(cuts), top_value / len(cuts))
        loudness = loudness * jnp.repeat(jnp.exp(heights), shape[dim] // shards_of).reshape((-1,) + (1,) * (len(shape) - 1 - dim))
    return loudness


def bell_draw(own_key, shape, spread, limit, shards=(), held_as=jnp.bfloat16):
    result = jax.random.normal(own_key, shape, jnp.float32) * spread
    if len(shards) > 0:
        result = steps_of(own_key, shape, shards, -0.22, 0.18) * result
    return jnp.clip(result, min=-limit, max=limit).astype(held_as)


def setup_inputs(seed: int = 0) -> dict:
    key_of = jax.random.split(jax.random.key(seed), 5)
    return {
        "density": bell_draw(key_of[0], (NB * BLK, NB * BLK), 0.3, 4.0, ((0, 4), (1, 8)), jnp.float32),
        "block_mask": draw_block_mask(jax.random.fold_in(key_of[4], 71), 0),
        "keep_mask": place_ends((jax.random.randint(key_of[2], (NB, NB), 0, 4) < 3).astype(jnp.int32), jax.random.fold_in(key_of[2], 1), 0, 1),
        "owner": draw_owner(jax.random.fold_in(key_of[4], 71), 0),
    }


def reference(density, block_mask, keep_mask, owner):
    stored = block_mask.astype(jnp.float32)[:, None, :, None]
    masked = (density.reshape(NB, BLK, NB, BLK) * stored).reshape(NB * BLK, NB * BLK)
    square = jnp.zeros_like(masked)
    for section_start in (0, (NB // 2) * BLK):
        span = BC * BLK
        square = square + jnp.dot(masked[:, section_start:section_start + span], masked[section_start:section_start + span, :], precision=lax.Precision.HIGHEST, preferred_element_type=jnp.float32)
    kept = keep_mask.astype(jnp.float32)[:, None, :, None]
    updated = (2.0 * masked - square).reshape(NB, BLK, NB, BLK) * kept
    listed = updated.reshape(N_ROW, BR, BLK, N_COL, BC, BLK).transpose(0, 3, 1, 4, 2, 5).reshape(DEVICES * TILE, BLK, BLK)
    order = jnp.argsort(owner, stable=True)
    return listed[order]
```

```python
import functools

import jax
import jax.numpy as jnp
from jax import lax
from jax.experimental import pallas as pl
from jax.experimental.pallas import tpu as pltpu
from jax.sharding import Mesh, PartitionSpec as P

NZS = 8
DEPTH = 8
OUT_SLOTS = 4


def near_square(count):
    first = 1
    while first * first < count:
        first *= 2
    return first, count // first


def pack_kernel(rows, cols, size, stored, mask_ref, density_ref, out_ref, sems):
    def visit(place, found):
        row = place // cols
        col = place % cols
        here = mask_ref[row, col] != 0

        @pl.when(here & (found < stored))
        def _():
            pltpu.make_async_copy(
                density_ref.at[pl.ds(row * size, size), pl.ds(col * size, size)],
                out_ref.at[found],
                sems.at[found],
            ).start()

        return found + here.astype(jnp.int32)

    lax.fori_loop(0, rows * cols, visit, jnp.int32(0))
    for slot in range(stored):
        pltpu.make_async_copy(
            density_ref.at[pl.ds(0, size), pl.ds(0, size)], out_ref.at[slot], sems.at[slot]
        ).wait()


def pack_stored(density, block_mask, size, stored):
    rows, cols = block_mask.shape
    return pl.pallas_call(
        functools.partial(pack_kernel, rows, cols, size, stored),
        out_shape=jax.ShapeDtypeStruct((stored, size, size), density.dtype),
        in_specs=[
            pl.BlockSpec(memory_space=pltpu.SMEM),
            pl.BlockSpec(memory_space=pl.ANY),
        ],
        out_specs=pl.BlockSpec(memory_space=pl.ANY),
        scratch_shapes=[pltpu.SemaphoreType.DMA((stored,))],
        name="pack_stored",
    )(block_mask, density)


def plan_rounds(depth, height, width):
    have = {(0, 0, 0)}
    shifts = sorted(range(1, depth), key=lambda s: (min(s, depth - s), s))
    busy, flying = 0, None
    rounds = []
    total = depth * height * width
    while len(have) < total or flying is not None:
        steps, arriving = [], []
        if busy == 0 and shifts:
            shift = shifts.pop(0)
            busy, flying = min(shift, depth - shift), (shift, 0, 0)
            steps.append(("z", shift, (0, 0, 0), flying))
        taken = set()
        for axis in ("x", "y"):
            options = []
            for s, dy, dx in have:
                target = (s, dy, dx + 1) if axis == "x" else (s, dy + 1, dx)
                if target[1] < height and target[2] < width and target not in have and target not in taken:
                    order = shift_order(depth).index(s)
                    options.append((target[1] > 0 and target[2] > 0, order, target, (s, dy, dx)))
            if options:
                _, _, target, source = min(options)
                taken.add(target)
                steps.append((axis, 1, source, target))
        arriving = list(taken)
        if busy:
            busy -= 1
            if busy == 0:
                arriving.append(flying)
                flying = None
        have.update(arriving)
        rounds.append((steps, arriving))
    return rounds


def shift_order(depth):
    return [0] + sorted(range(1, depth), key=lambda s: (min(s, depth - s), s))


def ring(axis, shift):
    count = lax.axis_size(axis)
    return [(i, (i + shift) % count) for i in range(count)]


def gather_pieces(own):
    depth, height, width = (lax.axis_size(a) for a in ("z", "y", "x"))
    pieces = {(0, 0, 0): own}
    pending = {}
    crossed = {}
    fresh = [(0, 0, 0)]
    for steps, arriving in plan_rounds(depth, height, width):
        for axis, shift, source, target in steps:
            pending[target] = lax.ppermute(pieces[source], axis, ring(axis, shift))
        for key in fresh:
            crossed[key] = lax.ppermute(pieces[key], "c", ring("c", 1))
        names = list(pieces) + arriving
        tied = lax.optimization_barrier([pieces.get(k, pending.get(k)) for k in names])
        pieces = dict(zip(names, tied))
        fresh = arriving
    for key in fresh:
        crossed[key] = lax.ppermute(pieces[key], "c", ring("c", 1))
    result = []
    for s in range(depth):
        for dy in range(height):
            for dx in range(width):
                result += [pieces[s, dy, dx], crossed[s, dy, dx]]
    return result


def choose(refs, piece, act):
    if len(refs) == 1:
        act(refs[0])
        return
    half = len(refs) // 2

    @pl.when(piece < half)
    def _():
        choose(refs[:half], piece, act)

    @pl.when(piece >= half)
    def _():
        choose(refs[half:], piece - half, act)


def update_kernel(layout, stored, table, *refs):
    pieces = refs[: layout["pieces"]]
    out_ref = refs[layout["pieces"] + 1]
    base, left, right, made, sem_base, sem_left, sem_right, sem_out = refs[layout["pieces"] + 2 :]
    picks = layout["picks"]
    active = table[layout["active"]]
    items = table[layout["items"]]

    def block_at(turn):
        return table[layout["order"] + jnp.minimum(turn, layout["tiles"] - 1)]

    def fetch(index, target, sem):
        choose(
            pieces,
            index // stored,
            lambda ref: pltpu.make_async_copy(ref.at[index % stored], target, sem).start(),
        )

    def arrived(target, sem):
        pltpu.make_async_copy(pieces[0].at[0], target, sem).wait()

    def load(item, turn, pick):
        slot = item % DEPTH
        block = block_at(turn)
        count = table[layout["counts"] + block]
        stored_at = table[layout["own"] + block]

        @pl.when(item < items)
        def _():
            @pl.when((pick == 0) & (stored_at >= 0))
            def _():
                fetch(stored_at, base.at[slot], sem_base.at[slot])

            @pl.when(count > 0)
            def _():
                fetch(table[layout["left"] + block * picks + pick], left.at[slot], sem_left.at[slot])
                fetch(table[layout["right"] + block * picks + pick], right.at[slot], sem_right.at[slot])

        return advance(turn, pick, count)

    def advance(turn, pick, count):
        more = pick + 1 < count
        return jnp.where(more, turn, turn + 1), jnp.where(more, pick + 1, 0)

    def send(turn):
        slot = turn % OUT_SLOTS
        return pltpu.make_async_copy(made.at[slot], out_ref.at[block_at(turn)], sem_out.at[slot])

    ahead = (jnp.int32(0), jnp.int32(0))
    for item in range(DEPTH):
        ahead = load(jnp.int32(item), *ahead)

    def step(item, carry):
        turn, pick, next_turn, next_pick = carry
        slot = item % DEPTH
        out_slot = turn % OUT_SLOTS
        block = block_at(turn)
        count = table[layout["counts"] + block]
        stored_at = table[layout["own"] + block]

        @pl.when(pick == 0)
        def _():
            @pl.when(turn >= OUT_SLOTS)
            def _():
                send(turn - OUT_SLOTS).wait()

            @pl.when(stored_at >= 0)
            def _():
                arrived(base.at[slot], sem_base.at[slot])
                made[out_slot] = 2.0 * base[slot]

            @pl.when(stored_at < 0)
            def _():
                made[out_slot] = jnp.zeros(made.shape[1:], made.dtype)

        @pl.when(count > 0)
        def _():
            arrived(left.at[slot], sem_left.at[slot])
            arrived(right.at[slot], sem_right.at[slot])
            made[out_slot] -= jnp.dot(
                left[slot],
                right[slot],
                precision=lax.Precision.HIGHEST,
                preferred_element_type=jnp.float32,
            )

        @pl.when(pick + 1 >= count)
        def _():
            send(turn).start()

        next_turn, next_pick = load(item + DEPTH, next_turn, next_pick)
        turn, pick = advance(turn, pick, count)
        return turn, pick, next_turn, next_pick

    lax.fori_loop(0, items, step, (jnp.int32(0), jnp.int32(0)) + ahead)
    for back in range(OUT_SLOTS):

        @pl.when(active > back)
        def _():
            send(active - 1 - back).wait()


def update_blocks(table, layout, pieces, zeros):
    stored, size, _ = pieces[0].shape
    block = (size, size)
    return pl.pallas_call(
        functools.partial(update_kernel, layout, stored),
        out_shape=jax.ShapeDtypeStruct(zeros.shape, zeros.dtype),
        in_specs=[pl.BlockSpec(memory_space=pltpu.SMEM)]
        + [pl.BlockSpec(memory_space=pl.ANY)] * (len(pieces) + 1),
        out_specs=pl.BlockSpec(memory_space=pl.ANY),
        scratch_shapes=[pltpu.VMEM((DEPTH,) + block, jnp.float32)] * 3
        + [pltpu.VMEM((OUT_SLOTS,) + block, jnp.float32)]
        + [pltpu.SemaphoreType.DMA((DEPTH,))] * 3
        + [pltpu.SemaphoreType.DMA((OUT_SLOTS,))],
        input_output_aliases={len(pieces) + 1: 0},
        name="update_owned",
    )(table, *pieces, zeros)


def work_table(masks, keeps, owners, sizes, band_rows, band_cols, stored):
    depth, height, width = sizes
    tiles = band_rows * band_cols
    rows, cols = height * 2, depth * width
    devices = rows * cols
    y, c, z, x = (lax.axis_index(a) for a in ("y", "c", "z", "x"))
    me = ((y * 2 + c) * depth + z) * width + x
    tile = lax.iota(jnp.int32, devices)
    tile_x = tile % width
    tile_z = tile // width % depth
    tile_c = tile // cols % 2
    tile_y = tile // cols // 2
    piece = (
        ((z - tile_z) % depth * height + (y - tile_y) % height) * width + (x - tile_x) % width
    ) * 2 + (c - tile_c) % 2
    ranks = jnp.cumsum(masks, axis=1) - 1
    slots = jnp.where(masks != 0, piece[:, None] * stored + ranks, -1)
    places = (
        slots.reshape(rows, cols, band_rows, band_cols)
        .transpose(0, 2, 1, 3)
        .reshape(rows * band_rows, cols * band_cols)
    )
    starts = [section * band_cols for section in (0, cols // 2)]
    left_places = jnp.concatenate([places[:, s : s + band_cols] for s in starts], axis=1)
    right_places = jnp.concatenate([places[s : s + band_cols, :] for s in starts], axis=0).T
    picks = left_places.shape[1]

    mine = (owners == me).reshape(-1)
    order = jnp.cumsum(mine.astype(jnp.int32)) - 1
    spots = lax.iota(jnp.int32, tiles)
    match = mine[None, :] & (order[None, :] == spots[:, None])
    pick_from = lambda values: jnp.sum(jnp.where(match, values.reshape(1, -1), 0), axis=1)
    listed = pick_from(lax.iota(jnp.int32, devices * tiles))
    kept = pick_from(keeps) != 0
    own = pick_from(slots)
    owner_tile, inside = listed // tiles, listed % tiles
    block_row = owner_tile // cols * band_rows + inside // band_cols
    block_col = owner_tile % cols * band_cols + inside % band_cols

    def rows_of(values, index):
        hit = index[:, None] == lax.iota(jnp.int32, values.shape[0])[None, :]
        return jnp.sum(jnp.where(hit[:, :, None], values[None], 0), axis=1)

    lefts = rows_of(left_places, block_row)
    rights = rows_of(right_places, block_col)
    valid = (lefts >= 0) & (rights >= 0) & kept[:, None]
    counts = jnp.sum(valid.astype(jnp.int32), axis=1)
    nth = jnp.cumsum(valid.astype(jnp.int32), axis=1) - 1
    put = valid[:, None, :] & (nth[:, None, :] == lax.iota(jnp.int32, picks)[None, :, None])
    lefts = jnp.sum(jnp.where(put, lefts[:, None, :], 0), axis=2)
    rights = jnp.sum(jnp.where(put, rights[:, None, :], 0), axis=2)
    active = kept & ((own >= 0) | (counts > 0))
    turns = jnp.cumsum(active.astype(jnp.int32)) - 1
    turn_match = active[None, :] & (turns[None, :] == spots[:, None])
    blocks = jnp.sum(jnp.where(turn_match, spots[None, :], 0), axis=1)
    items = jnp.sum(jnp.where(active, jnp.maximum(counts, 1), 0))
    totals = jnp.stack([jnp.sum(active.astype(jnp.int32)), items])
    parts = {"order": blocks, "own": own, "counts": counts, "left": lefts, "right": rights, "active": totals}
    layout, at = {"tiles": tiles, "picks": picks}, 0
    for name, part in parts.items():
        layout[name] = at
        at += part.size
    layout["items"] = layout["active"] + 1
    return jnp.concatenate([part.reshape(-1) for part in parts.values()]), layout


def shards(density, block_mask, keep_mask, owner):
    band_rows, band_cols = block_mask.shape
    size = density.shape[1] // band_cols
    stored = NZS * (band_rows // band_cols)
    tiles = band_rows * band_cols
    everyone = ("y", "c", "z", "x")
    sizes = tuple(lax.axis_size(a) for a in ("z", "y", "x"))
    devices = lax.axis_size(everyone)
    own = pack_stored(density, block_mask, size, stored)
    facts = jnp.stack([block_mask.reshape(-1), keep_mask.reshape(-1), owner])
    facts = lax.all_to_all(
        jnp.broadcast_to(facts[None], (devices,) + facts.shape), everyone, 0, 0, tiled=True
    )
    table, layout = work_table(
        facts[:, 0], facts[:, 1], facts[:, 2], sizes, band_rows, band_cols, stored
    )
    pieces = gather_pieces(own)
    layout["pieces"] = len(pieces)
    zeros = jnp.zeros((tiles, size, size), density.dtype)
    return update_blocks(table, layout, pieces, zeros)


def solution(mesh):
    row_count, col_count = mesh.shape["row"], mesh.shape["col"]
    depth, width = near_square(col_count)
    grid = Mesh(mesh.devices.reshape(row_count // 2, 2, depth, width), ("y", "c", "z", "x"))
    rows, cols = ("y", "c"), ("z", "x")
    return jax.shard_map(
        shards,
        mesh=grid,
        in_specs=(P(rows, cols), P(rows, cols), P(rows, cols), P(rows + cols)),
        out_specs=P(rows + cols, None, None),
        check_vma=False,
    )
```
